32 devices in a mesh: groups: 2 (over y), ep: 8 (over z, x), dp: 2 (over core).
Axes of the slice: x: 2, y: 2, z: 4, core: 2. Of those that a mesh axis runs over, the one named last changes fastest.
Arguments:
- out_grad: bfloat16 [4096, 2048], P(('groups', 'ep', 'dp')), parts along dimension 0, may hold values from -6 to 6
- gate_prob: float32 [4096, 8], P(('groups', 'ep', 'dp')), parts along dimension 0, may hold values from 0.05 to 0.5
- saved_hidden: bfloat16 [4096, 8, 768], P(('groups', 'ep', 'dp')), parts along dimension 0, may hold values from -6 to 6
- slot_weight: bfloat16 [16, 768, 2048], P(('ep', 'dp')), may hold values from -0.125 to 0.125
- pair_slot: int32 [4096, 8], P(('groups', 'ep', 'dp')), parts along dimension 0, may hold values from 0 to 15, all different within a row; in each aligned block of 128 rows (0 to 127, 128 to 255, ...) at most 80 rows name the same one
- slot_expert: int32 [32], P('groups'), parts along dimension 0, may hold values from 0 to 7, as said below
Outputs:
- hidden_grad: bfloat16 [4096, 8, 768], P(('groups', 'ep', 'dp')), parts along dimension 0
- left_gram: bfloat16 [16, 768, 768], P(('groups', 'ep'), 'dp'), parts along dimension 0
- right_gram: bfloat16 [16, 2048, 2048], P(('groups', 'ep'), 'dp'), parts along dimension 0
The draws below stay inside these ranges and needn't reach their ends.
There are 2 independent parts, one for each index of `groups`. The reference program is written for one: setup_inputs(seed, part) draws one part's arguments, and reference() takes and returns one part's arrays. A program takes and returns all parts, laid end to end along the dimension named above; an argument that names none is the same for every part. Nothing has to cross between parts.
Inputs may be any that keep to these rules, and one draw needn't show every extreme that they name: `pair_slot`: each token names 8 different slots; the tokens of one device name one slot at most 80 times. Two slots of a token may host the same expert. `slot_expert`: slot 2 e hosts expert e. Slot 2 e + 1 hosts expert e, or expert e - 1 when e is odd.
All inputs are finite; a program needn't handle non-finite values.
Results may differ from the reference program's by a relative error of at most 0.0065.
Values may be sent and summed in bfloat16 or wider, within the bound.
A program may use at most 128 MiB of HBM per device.

```python
import math
import jax
import jax.numpy as jnp
import numpy as np
from jax import lax

D = 2048
FF = 768
TOP = 8
TOK_DEV = 128
EXPERTS = 8
SLOTS = 16
TOKENS = 2048
MOST = 80


def draw_slot_expert(key, part):
    key = jax.random.fold_in(key, 11)
    experts_row = jnp.arange(EXPERTS, dtype=jnp.int32)
    shifted = jax.random.randint(key, (EXPERTS,), 0, 2).astype(jnp.int32) * (experts_row % 2)
    spare_host = experts_row - shifted
    return jnp.stack([experts_row, spare_host], axis=1).reshape(SLOTS)


def block_levels(stream_key, shape, pieces, smallest, largest):
    level = 1.0
    for dim, parts in pieces:
        steps = jax.random.uniform(jax.random.fold_in(jax.random.fold_in(stream_key, 6), dim), (parts,), jnp.float32, smallest / len(pieces), largest / len(pieces))
        level = level * jnp.repeat(jnp.exp(steps), shape[dim] // parts).reshape((-1,) + (1,) * (len(shape) - 1 - dim))
    return level


def deal_out(key, own, number, rows, number_of, top, bound, lean):
    sequence = jax.random.permutation(key, number_of)
    packed, ordinary = load_shares(number_of, rows * top, bound, lean, True), load_shares(number_of, rows * top, bound, lean, False)
    places = jnp.arange(number_of)

    def named(sizes, offset_by):
        used = int((sizes > 0).sum())
        fixed = max(1, used // 4)
        moved = fixed + (places - fixed + offset_by * (used - fixed)) % max(1, number_of - fixed)
        return jnp.zeros((number_of,), jnp.int32).at[sequence[jnp.where(places < fixed, places, moved)]].set(jnp.asarray(sizes, jnp.int32))

    sizes = jnp.where(number % 4 == 0, named(packed, number // 4), named(ordinary, number - number // 4 - 1))
    mixed = jax.random.permutation(jax.random.fold_in(own, 3), number_of)
    donor, sink = mixed[0:number_of // 2 * 2:2], mixed[1:number_of // 2 * 2:2]
    slack = jnp.minimum(sizes[donor] - 1, bound - sizes[sink]) // 2
    slack = jnp.where((donor == sequence[0]) | (sink == sequence[0]) | (sizes[sink] == 0), 0, jnp.maximum(slack, 0))
    moved = jax.random.randint(jax.random.fold_in(own, 4), (number_of // 2,), 0, 1 << 20) % (slack + 1)
    sizes = sizes.at[donor].add(-moved).at[sink].add(moved)
    items = jnp.searchsorted(jnp.cumsum(sizes), jnp.arange(rows * top), side="right").astype(jnp.int32)
    listing = items.reshape(top, rows).T
    listing = listing[jax.random.permutation(jax.random.fold_in(own, 1), rows)]
    offset_by = jax.random.randint(jax.random.fold_in(own, 2), (rows, 1), 0, top)
    return jnp.take_along_axis(listing, (jnp.arange(top)[None, :] + offset_by) % top, axis=1)


def load_shares(number_of, total, most, slope, full):
    portions = [(1 << 20) // math.isqrt(standing ** slope) + 1 for standing in range(1, number_of + 1)]
    largest = most if full else min(most, max(-(-total // number_of), total * portions[0] // sum(portions)))
    least = 1 if total - largest >= number_of - 1 else 0
    counts, surplus = [largest] + [least] * (number_of - 1), total - largest - least * (number_of - 1)
    while surplus > 0:
        movable = [i for i in range(1, number_of) if counts[i] < largest] or [i for i in range(1, number_of) if counts[i] < most]
        mass, left = sum([portions[i] for i in movable]), surplus
        for i in movable:
            addition = min(most - counts[i], max(1, left * portions[i] // mass), surplus)
            counts[i] = counts[i] + addition
            surplus = surplus - addition
    return np.array(counts)


def centred(stream_key, extent, spread, reach, shards=(), kind=jnp.bfloat16):
    result = spread * jax.random.normal(stream_key, extent, jnp.float32)
    if shards:
        result = result * block_levels(stream_key, extent, shards, -0.22, 0.18)
    return jnp.clip(result, -reach, reach).astype(kind)


def setup_inputs(seed: int = 0, part: int = 0) -> dict:
    seeds = jax.random.split(jax.random.key(seed), 7)
    part_splits = jax.random.split(jax.random.fold_in(seeds[6], part), 7)
    out_grad = centred(part_splits[0], (TOKENS, D), 1.0, 6.0, ((0, 16),))
    gate_prob = jnp.clip(jnp.exp(math.log(0.5) - 2.3025851 * jax.random.uniform(part_splits[1], (TOKENS, TOP), jnp.float32) ** block_levels(part_splits[1], (TOKENS, TOP), ((0, 16),), -0.2, 0.2)), 0.05, 0.5)
    saved_hidden = centred(part_splits[2], (TOKENS, TOP, FF), 1.0, 6.0, ((0, 16),))
    slot_weight = centred(seeds[3], (SLOTS, FF, D), D ** -0.5, 0.125, ((0, 16),))
    pair_slot_keys = jax.random.split(jax.random.fold_in(part_splits[4], 1), TOKENS // TOK_DEV)
    pair_slot_turns = jax.random.permutation(jax.random.fold_in(part_splits[4], 3), TOKENS // TOK_DEV)
    pair_slot = jax.vmap(lambda own, number: deal_out(jax.random.fold_in(part_splits[4], 2), own, number, TOK_DEV, SLOTS, TOP, MOST, 2))(pair_slot_keys, pair_slot_turns).reshape((TOKENS, TOP))
    slot_expert = draw_slot_expert(jax.random.fold_in(jax.random.fold_in(seeds[6], part), 71), part)
    return {"out_grad": out_grad, "gate_prob": gate_prob, "saved_hidden": saved_hidden, "slot_weight": slot_weight, "pair_slot": pair_slot, "slot_expert": slot_expert}


def reference(out_grad, gate_prob, saved_hidden, slot_weight, pair_slot, slot_expert):
    npairs = TOKENS * TOP
    capacity = SLOTS * MOST
    target = pair_slot.reshape(npairs).astype(jnp.int32)
    gate_flat = gate_prob.reshape(npairs)
    hidden_flat = saved_hidden.reshape(npairs, FF)
    pair_index = jnp.arange(npairs, dtype=jnp.int32)

    def serve(slot):
        chosen = target == slot
        position = jnp.cumsum(chosen.astype(jnp.int32)) - 1
        position = jnp.where(chosen, position, capacity).astype(jnp.int32)
        source = jnp.full((capacity,), npairs, jnp.int32).at[position].set(pair_index, mode="drop")
        filled = source < npairs
        clipped = jnp.minimum(source, npairs - 1)
        scaled = out_grad[clipped // TOP].astype(jnp.float32) * gate_flat[clipped][:, None]
        grad_rows = jnp.where(filled[:, None], scaled, jnp.zeros((), jnp.float32)).astype(jnp.bfloat16)
        held_rows = jnp.where(filled[:, None], hidden_flat[clipped], jnp.zeros((), jnp.bfloat16))
        input_grads = lax.dot_general(grad_rows, slot_weight[slot], (((1,), (1,)), ((), ())),
                                      preferred_element_type=jnp.float32).astype(jnp.bfloat16)
        partial_value = lax.dot_general(held_rows, grad_rows, (((0,), (0,)), ((), ())),
                                  preferred_element_type=jnp.float32).astype(jnp.bfloat16)
        return input_grads, source, partial_value

    input_grads, sources, partials = lax.map(serve, jnp.arange(SLOTS, dtype=jnp.int32))
    collected = jnp.zeros((npairs + 1, FF), jnp.bfloat16)
    collected = collected.at[sources.reshape(-1)].set(input_grads.reshape(-1, FF))
    hidden_grad = collected[:npairs].reshape(TOKENS, TOP, FF)

    def add_slot(slot, total):
        return total.at[slot_expert[slot]].add(partials[slot].astype(jnp.float32))

    expert_grad = lax.fori_loop(0, SLOTS, add_slot, jnp.zeros((EXPERTS, FF, D), jnp.float32))

    def grams(block):
        rounded = block.astype(jnp.bfloat16)
        left = lax.dot_general(rounded, rounded, (((1,), (1,)), ((), ())),
                               preferred_element_type=jnp.float32) / D
        right = lax.dot_general(rounded, rounded, (((0,), (0,)), ((), ())),
                                preferred_element_type=jnp.float32) / FF
        return left.astype(jnp.bfloat16), right.astype(jnp.bfloat16)

    left_gram, right_gram = lax.map(grams, expert_grad)
    return hidden_grad, left_gram, right_gram
```

```python
import jax
import jax.numpy as jnp
from jax import lax
from jax.sharding import PartitionSpec as P

AXES = ("ep", "dp")
BLOCK = 16


def combined(gate_prob, expert_of_pair, saved_hidden, experts):
    tokens, choose = gate_prob.shape
    width = saved_hidden.shape[2]
    blocks = tokens // BLOCK
    pairs = BLOCK * choose
    gates = gate_prob.reshape(blocks, 1, 1, pairs)
    hosts = expert_of_pair.reshape(blocks, 1, 1, pairs)
    owner = jnp.arange(pairs, dtype=jnp.int32) // choose
    keep = (hosts == jnp.arange(experts, dtype=jnp.int32)[None, :, None, None]) & (
        owner[None, None, None, :] == jnp.arange(BLOCK, dtype=jnp.int32)[None, None, :, None]
    )
    high = lax.reduce_precision(gates, 8, 7)
    low = gates - high
    zero = jnp.zeros((), jnp.float32)
    weights = jnp.concatenate(
        [jnp.where(keep, high, zero), jnp.where(keep, low, zero)], axis=3
    ).astype(jnp.bfloat16)
    hidden = saved_hidden.reshape(blocks, pairs, width)
    hidden = jnp.concatenate([hidden, hidden], axis=1)
    out = lax.dot_general(
        weights.reshape(blocks, experts * BLOCK, 2 * pairs),
        hidden,
        (((2,), (1,)), ((0,), (0,))),
        preferred_element_type=jnp.float32,
    ).astype(jnp.bfloat16)
    return out.reshape(blocks, experts, BLOCK, width).transpose(1, 0, 2, 3).reshape(
        experts, tokens, width
    )


def local(out_grad, gate_prob, saved_hidden, slot_weight, pair_slot, slot_expert):
    tokens, choose = pair_slot.shape
    width = out_grad.shape[1]
    hidden_width = saved_hidden.shape[2]
    slot_count = slot_expert.shape[0]
    ep_count = lax.axis_size("ep")
    dp_count = lax.axis_size("dp")
    half = hidden_width // dp_count
    capacity = max(2, 5 * tokens * choose // (4 * slot_count))
    dp_index = lax.axis_index("dp")

    everyone = lax.all_gather(out_grad, AXES, axis=0, tiled=True)

    slots = jnp.arange(slot_count, dtype=jnp.int32)
    named = pair_slot[:, :, None] == slots[None, None, :]
    dense_gate = jnp.sum(jnp.where(named, gate_prob[:, :, None], 0.0), axis=1).T
    gates = lax.all_to_all(dense_gate, AXES, split_axis=0, concat_axis=0, tiled=True)

    expert_of_pair = jnp.sum(jnp.where(named, slot_expert[None, None, :], 0), axis=2)
    sums = combined(gate_prob, expert_of_pair, saved_hidden, ep_count)
    sums = (
        sums.reshape(ep_count, tokens, dp_count, half)
        .transpose(0, 2, 1, 3)
        .reshape(slot_count, tokens, half)
    )
    sums = lax.all_to_all(sums, AXES, split_axis=0, concat_axis=0, tiled=True)

    used = gates > 0
    before = (
        jnp.arange(tokens)[:, None] < jnp.arange(tokens)[None, :]
    ).astype(jnp.bfloat16)
    place = lax.dot_general(
        used.astype(jnp.bfloat16), before, (((1,), (0,)), ((), ())),
        preferred_element_type=jnp.float32,
    ).astype(jnp.int32)
    place = jnp.where(used, place, -1)
    select = place[:, None, :] == jnp.arange(capacity, dtype=jnp.int32)[None, :, None]
    rows = lax.dot_general(
        select.astype(jnp.bfloat16),
        everyone.reshape(slot_count, tokens, width),
        (((2,), (1,)), ((0,), (0,))),
        preferred_element_type=jnp.float32,
    )
    row_gate = jnp.sum(jnp.where(select, gates[:, None, :], 0.0), axis=2)
    pair_grad = (rows * row_gate[:, :, None]).astype(jnp.bfloat16)
    input_grads = lax.dot_general(
        pair_grad.reshape(slot_count * capacity, width),
        slot_weight[0],
        (((1,), (1,)), ((), ())),
        preferred_element_type=jnp.float32,
    ).astype(jnp.bfloat16)
    returned = lax.all_to_all(
        input_grads.reshape(slot_count, capacity, hidden_width),
        AXES, split_axis=0, concat_axis=0, tiled=True,
    )

    grad_half = lax.dot_general(
        sums.reshape(slot_count * tokens, half),
        everyone,
        (((0,), (0,)), ((), ())),
        preferred_element_type=jnp.float32,
    ).astype(jnp.bfloat16)
    rounded = lax.all_gather(grad_half, "dp", axis=0, tiled=True)
    left = (
        lax.dot_general(
            grad_half, rounded, (((1,), (1,)), ((), ())), preferred_element_type=jnp.float32
        )
        / width
    )
    width_rows = width // dp_count
    right_cols = lax.dynamic_slice_in_dim(rounded, dp_index * width_rows, width_rows, 1)
    right = (
        lax.dot_general(
            right_cols, rounded, (((0,), (0,)), ((), ())), preferred_element_type=jnp.float32
        )
        / hidden_width
    )

    served = jnp.any(named, axis=1).astype(jnp.bfloat16)
    earlier = lax.dot_general(
        before, served, (((0,), (0,)), ((), ())), preferred_element_type=jnp.float32
    ).astype(jnp.int32)
    position = jnp.sum(
        jnp.where(named, (earlier + slots * capacity)[:, None, :], 0), axis=2
    ).reshape(tokens * choose)
    pick = (
        position[:, None] == jnp.arange(slot_count * capacity, dtype=jnp.int32)[None, :]
    ).astype(jnp.bfloat16)
    hidden_grad = lax.dot_general(
        pick,
        returned.reshape(slot_count * capacity, hidden_width),
        (((1,), (0,)), ((), ())),
        preferred_element_type=jnp.float32,
    ).astype(jnp.bfloat16).reshape(tokens, choose, hidden_width)
    return (hidden_grad, left.astype(jnp.bfloat16)[None], right.astype(jnp.bfloat16)[None])


def solution(mesh):
    return jax.shard_map(
        local,
        mesh=mesh,
        in_specs=(
            P(("groups", "ep", "dp"), None),
            P(("groups", "ep", "dp"), None),
            P(("groups", "ep", "dp"), None, None),
            P(("ep", "dp"), None, None),
            P(("groups", "ep", "dp"), None),
            P("groups"),
        ),
        out_specs=(
            P(("groups", "ep", "dp"), None, None),
            P(("groups", "ep"), "dp", None),
            P(("groups", "ep"), "dp", None),
        ),
        check_vma=False,
    )
```

```python
import functools
import jax
import jax.numpy as jnp
from jax import lax
from jax.experimental import pallas as pl
from jax.experimental.pallas import tpu as pltpu
from jax.sharding import PartitionSpec as P

AXES = ("ep", "dp")
BLOCK = 16


def combined(gate_prob, expert_of_pair, saved_hidden, experts):
    tokens, choose = gate_prob.shape
    width = saved_hidden.shape[2]
    blocks = tokens // BLOCK
    pairs = BLOCK * choose
    gates = gate_prob.reshape(blocks, 1, 1, pairs)
    hosts = expert_of_pair.reshape(blocks, 1, 1, pairs)
    owner = jnp.arange(pairs, dtype=jnp.int32) // choose
    keep = (hosts == jnp.arange(experts, dtype=jnp.int32)[None, :, None, None]) & (
        owner[None, None, None, :] == jnp.arange(BLOCK, dtype=jnp.int32)[None, None, :, None]
    )
    high = lax.reduce_precision(gates, 8, 7)
    low = gates - high
    zero = jnp.zeros((), jnp.float32)
    weights = jnp.concatenate(
        [jnp.where(keep, high, zero), jnp.where(keep, low, zero)], axis=3
    ).astype(jnp.bfloat16)
    hidden = saved_hidden.reshape(blocks, pairs, width)
    hidden = jnp.concatenate([hidden, hidden], axis=1)
    out = lax.dot_general(
        weights.reshape(blocks, experts * BLOCK, 2 * pairs),
        hidden,
        (((2,), (1,)), ((0,), (0,))),
        preferred_element_type=jnp.float32,
    ).astype(jnp.bfloat16)
    return out.reshape(blocks, experts, BLOCK, width).transpose(1, 0, 2, 3).reshape(
        experts, tokens, width
    )


def local(out_grad, gate_prob, saved_hidden, slot_weight, pair_slot, slot_expert):
    tokens, choose = pair_slot.shape
    width = out_grad.shape[1]
    hidden_width = saved_hidden.shape[2]
    slot_count = slot_expert.shape[0]
    ep_count = lax.axis_size("ep")
    dp_count = lax.axis_size("dp")
    half = hidden_width // dp_count
    capacity = max(2, 5 * tokens * choose // (4 * slot_count))
    dp_index = lax.axis_index("dp")

    everyone = lax.all_gather(out_grad, AXES, axis=0, tiled=True)

    slots = jnp.arange(slot_count, dtype=jnp.int32)
    named = pair_slot[:, :, None] == slots[None, None, :]
    dense_gate = jnp.sum(jnp.where(named, gate_prob[:, :, None], 0.0), axis=1).T
    gates = lax.all_to_all(dense_gate, AXES, split_axis=0, concat_axis=0, tiled=True)

    expert_of_pair = jnp.sum(jnp.where(named, slot_expert[None, None, :], 0), axis=2)
    sums = combined(gate_prob, expert_of_pair, saved_hidden, ep_count)
    sums = (
        sums.reshape(ep_count, tokens, dp_count, half)
        .transpose(0, 2, 1, 3)
        .reshape(slot_count, tokens, half)
    )
    sums = lax.all_to_all(sums, AXES, split_axis=0, concat_axis=0, tiled=True)

    used = gates > 0
    before = (
        jnp.arange(tokens)[:, None] < jnp.arange(tokens)[None, :]
    ).astype(jnp.bfloat16)
    place = lax.dot_general(
        used.astype(jnp.bfloat16), before, (((1,), (0,)), ((), ())),
        preferred_element_type=jnp.float32,
    ).astype(jnp.int32)
    place = jnp.where(used, place, -1)
    select = place[:, None, :] == jnp.arange(capacity, dtype=jnp.int32)[None, :, None]
    rows = lax.dot_general(
        select.astype(jnp.bfloat16),
        everyone.reshape(slot_count, tokens, width),
        (((2,), (1,)), ((0,), (0,))),
        preferred_element_type=jnp.float32,
    )
    row_gate = jnp.sum(jnp.where(select, gates[:, None, :], 0.0), axis=2)
    pair_grad = (rows * row_gate[:, :, None]).astype(jnp.bfloat16)
    input_grads = lax.dot_general(
        pair_grad.reshape(slot_count * capacity, width),
        slot_weight[0],
        (((1,), (1,)), ((), ())),
        preferred_element_type=jnp.float32,
    ).astype(jnp.bfloat16)
    returned = lax.all_to_all(
        input_grads.reshape(slot_count, capacity, hidden_width),
        AXES, split_axis=0, concat_axis=0, tiled=True,
    )

    grad_half = lax.dot_general(
        sums.reshape(slot_count * tokens, half),
        everyone,
        (((0,), (0,)), ((), ())),
        preferred_element_type=jnp.float32,
    ).astype(jnp.bfloat16)
    rounded = lax.all_gather(grad_half, "dp", axis=0, tiled=True)
    left = (
        lax.dot_general(
            grad_half, rounded, (((1,), (1,)), ((), ())), preferred_element_type=jnp.float32
        )
        / width
    )
    width_rows = width // dp_count
    right_cols = lax.dynamic_slice_in_dim(rounded, dp_index * width_rows, width_rows, 1)
    right = (
        lax.dot_general(
            right_cols, rounded, (((0,), (0,)), ((), ())), preferred_element_type=jnp.float32
        )
        / hidden_width
    )

    served = jnp.any(named, axis=1).astype(jnp.bfloat16)
    earlier = lax.dot_general(
        before, served, (((0,), (0,)), ((), ())), preferred_element_type=jnp.float32
    ).astype(jnp.int32)
    position = jnp.sum(
        jnp.where(named, (earlier + slots * capacity)[:, None, :], 0), axis=2
    ).reshape(tokens * choose)
    pick = (
        position[:, None] == jnp.arange(slot_count * capacity, dtype=jnp.int32)[None, :]
    ).astype(jnp.bfloat16)
    hidden_grad = lax.dot_general(
        pick,
        returned.reshape(slot_count * capacity, hidden_width),
        (((1,), (0,)), ((), ())),
        preferred_element_type=jnp.float32,
    ).astype(jnp.bfloat16).reshape(tokens, choose, hidden_width)
    return (hidden_grad, left.astype(jnp.bfloat16)[None], right.astype(jnp.bfloat16)[None])


def exchange_kernel(
    ep_count, dp_count, capacity,
    grad_hbm, hidden_hbm, weight_hbm, gate_out, gate_pairs, host_pairs,
    ret_hbm, left_hbm, right_hbm,
    shards, weight, hidden, gate_in, place, sum_out, sum_in, sum_t, rows, ret_out,
    full, cols_t, left, right,
    local_sem, out_sem, o_send, o_recv, g_send, g_recv, c_send, c_recv, r_send, r_recv, x_send, x_recv,
):
    e = lax.axis_index("ep")
    c = lax.axis_index("dp")
    z, x = e // 2, e % 2
    lines = ep_count // 2
    count = ep_count * dp_count
    me = e * dp_count + c
    tokens, width = shards.shape[1:]
    hidden_width = weight.shape[0]
    half = hidden_width // dp_count

    def at(device):
        return {"ep": device // dp_count, "dp": device % dp_count}

    def index(line, column, core):
        return (line * 2 + column) * dp_count + core

    def remote(src, dst, send, recv, device):
        return pltpu.make_async_remote_copy(
            src_ref=src, dst_ref=dst, send_sem=send, recv_sem=recv,
            device_id=at(device), device_id_type=pl.DeviceIdType.MESH,
        )

    def each_peer(body):
        def step(d, carry):
            body(lax.rem(me + d, count))
            return carry
        lax.fori_loop(1, count, step, 0)

    loads = [
        pltpu.make_async_copy(grad_hbm, shards.at[me], local_sem.at[0]),
        pltpu.make_async_copy(hidden_hbm, hidden, local_sem.at[1]),
        pltpu.make_async_copy(weight_hbm, weight, local_sem.at[2]),
    ]
    for load in loads:
        load.start()

    barrier = pltpu.get_barrier_semaphore()
    each_peer(lambda peer: pl.semaphore_signal(
        barrier, inc=1, device_id=at(peer), device_id_type=pl.DeviceIdType.MESH))
    pl.semaphore_wait(barrier, count - 1)

    def gate_copy(peer):
        return remote(gate_out.at[peer], gate_in.at[me], g_send.at[peer], g_recv.at[me], peer)

    def sum_copy(peer):
        return remote(sum_out.at[peer], sum_in.at[me], c_send.at[peer], c_recv.at[me], peer)

    def ret_copy(peer):
        return remote(ret_out.at[peer], ret_hbm.at[me], r_send.at[peer], r_recv.at[me], peer)

    def shard_copy(route, shard, device):
        return remote(shards.at[shard], shards.at[shard], o_send.at[route, shard], o_recv.at[shard], device)

    def wait_shard(shard):
        shard_copy(0, shard, (me + 1) % count).wait_recv()

    def relay(line, action):
        shard = index(line, x, c)

        @pl.when((line <= z) & (z + 1 < lines))
        def _():
            action(shard_copy(0, shard, index(z + 1, x, c)))

        @pl.when((line >= z) & (z >= 1))
        def _():
            action(shard_copy(1, shard, index(z - 1, x, c)))

        action(shard_copy(2, shard, index(z, 1 - x, c)))
        action(shard_copy(3, shard, index(z, x, 1 - c)))

    def cross(line, action):
        action(shard_copy(3, index(line, 1 - x, c), index(z, x, 1 - c)))

    start = lambda copy: copy.start()
    each_peer(lambda peer: gate_copy(peer).start())
    loads[0].wait()
    relay(z, start)
    gate_in[me] = gate_out[me]

    loads[1].wait()
    block = gate_pairs.shape[2]
    per = tokens // gate_pairs.shape[0]
    choose = block // per
    line_of = lax.broadcasted_iota(jnp.int32, (ep_count * per, block), 0)
    lane_of = lax.broadcasted_iota(jnp.int32, (ep_count * per, block), 1)
    own = (lane_of // choose) == (line_of % per)

    def sum_block(b, carry):
        keep = own & (host_pairs[b] == line_of // per)
        exact = jnp.where(keep, gate_pairs[b], 0.0)
        high = exact.astype(jnp.bfloat16)
        low = (exact - high.astype(jnp.float32)).astype(jnp.bfloat16)
        values = hidden[pl.ds(pl.multiple_of(b * block, block), block), :]
        out = jnp.dot(high, values, preferred_element_type=jnp.float32)
        out = (out + jnp.dot(low, values, preferred_element_type=jnp.float32)).astype(jnp.bfloat16)
        for host in range(ep_count):
            for core in range(dp_count):
                sum_out[host * dp_count + core, pl.ds(pl.multiple_of(b * per, per), per), :] = out[
                    host * per:(host + 1) * per, core * half:(core + 1) * half]
        return carry

    lax.fori_loop(0, gate_pairs.shape[0], sum_block, 0)
    own_sum = pltpu.make_async_copy(sum_out.at[me], sum_in.at[me], local_sem.at[1])
    own_sum.start()
    each_peer(lambda peer: sum_copy(peer).start())

    each_peer(lambda peer: gate_copy(peer).wait_send())
    each_peer(lambda peer: remote(
        gate_out.at[peer], gate_in.at[peer], g_send.at[peer], g_recv.at[peer], peer).wait_recv())
    gates = gate_in[:, 0, :]
    used = gates > 0
    before = (
        lax.broadcasted_iota(jnp.int32, (tokens, tokens), 0)
        < lax.broadcasted_iota(jnp.int32, (tokens, tokens), 1)
    ).astype(jnp.float32).astype(jnp.bfloat16)
    earlier = jnp.dot(
        used.astype(jnp.float32).astype(jnp.bfloat16), before, preferred_element_type=jnp.float32)
    place[:, 0, :] = jnp.where(used, earlier, -1.0)
    loads[2].wait()

    rank = lax.broadcasted_iota(jnp.int32, (capacity, tokens), 0).astype(jnp.float32)
    tile = 256

    def serve(line):
        first = index(line, 0, 0)
        number = 2 * dp_count

        def gather(i, carry):
            shard = first + i
            select = place[shard] == rank
            picked = jnp.dot(
                jnp.where(select, 1.0, 0.0).astype(jnp.bfloat16), shards[shard],
                preferred_element_type=jnp.float32)
            gate = jnp.sum(jnp.where(select, gate_in[shard], 0.0), axis=1, keepdims=True)
            rows[i] = (picked * gate).astype(jnp.bfloat16)
            return carry

        lax.fori_loop(0, number, gather, 0)

        def product(n, carry):
            lanes = pl.ds(pl.multiple_of(n * tile, tile), tile)
            out = lax.dot_general(
                rows[...].reshape(number * capacity, width), weight[lanes, :],
                (((1,), (1,)), ((), ())), preferred_element_type=jnp.float32)
            ret_out[pl.ds(first, number), :, lanes] = out.astype(jnp.bfloat16).reshape(
                number, capacity, tile)
            return carry

        lax.fori_loop(0, hidden_width // tile, product, 0)

        def send(i, carry):
            shard = first + i

            @pl.when(shard != me)
            def _():
                ret_copy(shard).start()

            @pl.when(shard == me)
            def _():
                pltpu.make_async_copy(ret_out.at[me], ret_hbm.at[me], local_sem.at[0]).start()

            return carry

        lax.fori_loop(0, number, send, 0)

    def inside(line, body):
        @pl.when((line >= 0) & (line < lines))
        def _():
            body(line)

    def take_line(line):
        wait_shard(index(line, x, c))
        relay(line, start)

    def take_cross(line):
        wait_shard(index(line, 1 - x, c))
        cross(line, start)

    side = 1 - 2 * (z // 2)
    second = z + side
    fourth = 3 * (1 - z // 2)
    order = [z, second, 6 - z - second - fourth, fourth]
    for level in range(1, lines + 1):
        if level < lines:
            inside(z - level, take_line)
            inside(z + level, take_line)
        if level == 1:
            take_cross(z)
        else:
            inside(z - level + 1, take_cross)
            inside(z + level - 1, take_cross)
        line = order[level - 1]
        wait_shard(index(line, 0, 1 - c))
        wait_shard(index(line, 1, 1 - c))
        serve(line)

    own_sum.wait()
    each_peer(lambda peer: remote(
        sum_out.at[peer], sum_in.at[peer], c_send.at[peer], c_recv.at[peer], peer).wait_recv())

    def turn(j, carry):
        sum_t[:, pl.ds(pl.multiple_of(j * tokens, tokens), tokens)] = sum_in[j].T
        return carry

    lax.fori_loop(0, count, turn, 0)
    mine = pl.ds(pl.multiple_of(c * half, half), half)

    def grad_tile(n, carry):
        lanes = pl.ds(pl.multiple_of(n * tile, tile), tile)
        full[mine, lanes] = jnp.dot(
            sum_t[...], shards[:, :, lanes].reshape(count * tokens, tile),
            preferred_element_type=jnp.float32).astype(jnp.bfloat16)
        return carry

    lax.fori_loop(0, width // tile, grad_tile, 0)
    swap = remote(full.at[mine], full.at[mine], x_send, x_recv, index(z, x, 1 - c))
    swap.start()
    swap.wait()

    part = width // dp_count
    cols_t[...] = full[:, pl.ds(pl.multiple_of(c * part, part), part)].T
    left[...] = (
        lax.dot_general(
            full[mine, :], full[...], (((1,), (1,)), ((), ())), preferred_element_type=jnp.float32)
        / width
    ).astype(jnp.bfloat16)
    left_copy = pltpu.make_async_copy(left, left_hbm, out_sem.at[0])
    left_copy.start()

    def right_tile(n, carry):
        lanes = pl.ds(pl.multiple_of(n * tile, tile), tile)
        right[:, lanes] = (
            jnp.dot(cols_t[...], full[:, lanes], preferred_element_type=jnp.float32) / hidden_width
        ).astype(jnp.bfloat16)
        return carry

    lax.fori_loop(0, width // tile, right_tile, 0)
    right_copy = pltpu.make_async_copy(right, right_hbm, out_sem.at[1])
    right_copy.start()

    each_peer(lambda peer: remote(
        ret_out.at[peer], ret_hbm.at[peer], r_send.at[peer], r_recv.at[peer], peer).wait_recv())
    pltpu.make_async_copy(ret_out.at[me], ret_hbm.at[me], local_sem.at[0]).wait()
    each_peer(lambda peer: sum_copy(peer).wait_send())
    each_peer(lambda peer: ret_copy(peer).wait_send())
    wait_send = lambda copy: copy.wait_send()
    for line in range(lines):
        relay(line, wait_send)
        cross(line, wait_send)
    left_copy.wait()
    right_copy.wait()


def exchange(out_grad, saved_hidden, weight, dense_gate, gate_pairs, host_pairs, ep_count, dp_count, capacity):
    tokens, width = out_grad.shape
    pairs, hidden_width = saved_hidden.shape
    count = ep_count * dp_count
    half, part = hidden_width // dp_count, width // dp_count
    bf16, f32 = jnp.bfloat16, jnp.float32
    dma = pltpu.SemaphoreType.DMA
    anywhere = pl.BlockSpec(memory_space=pl.ANY)
    vmem = pl.BlockSpec(memory_space=pltpu.VMEM)
    return pl.pallas_call(
        functools.partial(exchange_kernel, ep_count, dp_count, capacity),
        out_shape=(
            jax.ShapeDtypeStruct((count, capacity, hidden_width), bf16),
            jax.ShapeDtypeStruct((half, hidden_width), bf16),
            jax.ShapeDtypeStruct((part, width), bf16),
        ),
        in_specs=[anywhere] * 3 + [vmem] * 3,
        out_specs=(anywhere,) * 3,
        scratch_shapes=[
            pltpu.VMEM((count, tokens, width), bf16),
            pltpu.VMEM((hidden_width, width), bf16),
            pltpu.VMEM((pairs, hidden_width), bf16),
            pltpu.VMEM((count, 1, tokens), f32),
            pltpu.VMEM((count, 1, tokens), f32),
            pltpu.VMEM((count, tokens, half), bf16),
            pltpu.VMEM((count, tokens, half), bf16),
            pltpu.VMEM((half, count * tokens), bf16),
            pltpu.VMEM((2 * dp_count, capacity, width), bf16),
            pltpu.VMEM((count, capacity, hidden_width), bf16),
            pltpu.VMEM((hidden_width, width), bf16),
            pltpu.VMEM((part, hidden_width), bf16),
            pltpu.VMEM((half, hidden_width), bf16),
            pltpu.VMEM((part, width), bf16),
            dma((3,)), dma((2,)), dma((4, count)), dma((count,)), dma((count,)), dma((count,)),
            dma((count,)), dma((count,)), dma((count,)), dma((count,)), dma, dma,
        ],
        compiler_params=pltpu.CompilerParams(
            collective_id=0, has_side_effects=True, vmem_limit_bytes=56 << 20),
        cost_estimate=pl.CostEstimate(
            flops=16_000_000_000, bytes_accessed=20_000_000, transcendentals=0),
    )(out_grad, saved_hidden, weight, dense_gate, gate_pairs, host_pairs)


def restore(returned, named, before, capacity):
    tokens, choose, slot_count = named.shape
    hidden_width = returned.shape[2]
    slots = jnp.arange(slot_count, dtype=jnp.int32)
    served = jnp.any(named, axis=1).astype(jnp.bfloat16)
    earlier = lax.dot_general(
        before, served, (((0,), (0,)), ((), ())), preferred_element_type=jnp.float32
    ).astype(jnp.int32)
    position = jnp.sum(
        jnp.where(named, (earlier + slots * capacity)[:, None, :], 0), axis=2
    ).reshape(tokens * choose)
    pick = (
        position[:, None] == jnp.arange(slot_count * capacity, dtype=jnp.int32)[None, :]
    ).astype(jnp.bfloat16)
    return lax.dot_general(
        pick,
        returned.reshape(slot_count * capacity, hidden_width),
        (((1,), (0,)), ((), ())),
        preferred_element_type=jnp.float32,
    ).astype(jnp.bfloat16).reshape(tokens, choose, hidden_width)


def fused(out_grad, gate_prob, saved_hidden, slot_weight, pair_slot, slot_expert):
    tokens, choose = pair_slot.shape
    slot_count = slot_expert.shape[0]
    ep_count = lax.axis_size("ep")
    dp_count = lax.axis_size("dp")
    capacity = max(2, 5 * tokens * choose // (4 * slot_count))
    slots = jnp.arange(slot_count, dtype=jnp.int32)
    named = pair_slot[:, :, None] == slots[None, None, :]
    dense_gate = jnp.sum(jnp.where(named, gate_prob[:, :, None], 0.0), axis=1).T
    expert_of_pair = jnp.sum(jnp.where(named, slot_expert[None, None, :], 0), axis=2)
    blocks = tokens // BLOCK
    returned, left, right = exchange(
        out_grad,
        saved_hidden.reshape(tokens * choose, saved_hidden.shape[2]),
        slot_weight[0],
        dense_gate[:, None, :],
        gate_prob.reshape(blocks, 1, BLOCK * choose),
        expert_of_pair.reshape(blocks, 1, BLOCK * choose),
        ep_count, dp_count, capacity,
    )
    before = (
        jnp.arange(tokens)[:, None] < jnp.arange(tokens)[None, :]
    ).astype(jnp.bfloat16)
    return restore(returned, named, before, capacity), left[None], right[None]


def solution(mesh):
    fits = mesh.shape["ep"] == 8 and mesh.shape["dp"] == 2
    return jax.shard_map(
        fused if fits else local,
        mesh=mesh,
        in_specs=(
            P(("groups", "ep", "dp"), None),
            P(("groups", "ep", "dp"), None),
            P(("groups", "ep", "dp"), None, None),
            P(("ep", "dp"), None, None),
            P(("groups", "ep", "dp"), None),
            P("groups"),
        ),
        out_specs=(
            P(("groups", "ep", "dp"), None, None),
            P(("groups", "ep"), "dp", None),
            P(("groups", "ep"), "dp", None),
        ),
        check_vma=False,
    )
```

```python
import functools
import jax
import jax.numpy as jnp
from jax import lax
from jax.experimental import pallas as pl
from jax.experimental.pallas import tpu as pltpu
from jax.sharding import PartitionSpec as P

AXES = ("ep", "dp")
BLOCK = 16
CHUNKS = 2
PLAN = (
    ("line cross", 1), ("across", 0), ("serve", 0),
    ("line cross", 2), ("serve", 1), ("near", 0),
    ("line cross", 3), ("serve", 2),
    ("cross", 4), ("serve", 3),
)


def combined(gate_prob, expert_of_pair, saved_hidden, experts):
    tokens, choose = gate_prob.shape
    width = saved_hidden.shape[2]
    blocks = tokens // BLOCK
    pairs = BLOCK * choose
    gates = gate_prob.reshape(blocks, 1, 1, pairs)
    hosts = expert_of_pair.reshape(blocks, 1, 1, pairs)
    owner = jnp.arange(pairs, dtype=jnp.int32) // choose
    keep = (hosts == jnp.arange(experts, dtype=jnp.int32)[None, :, None, None]) & (
        owner[None, None, None, :] == jnp.arange(BLOCK, dtype=jnp.int32)[None, None, :, None]
    )
    high = lax.reduce_precision(gates, 8, 7)
    low = gates - high
    zero = jnp.zeros((), jnp.float32)
    weights = jnp.concatenate(
        [jnp.where(keep, high, zero), jnp.where(keep, low, zero)], axis=3
    ).astype(jnp.bfloat16)
    hidden = saved_hidden.reshape(blocks, pairs, width)
    hidden = jnp.concatenate([hidden, hidden], axis=1)
    out = lax.dot_general(
        weights.reshape(blocks, experts * BLOCK, 2 * pairs),
        hidden,
        (((2,), (1,)), ((0,), (0,))),
        preferred_element_type=jnp.float32,
    ).astype(jnp.bfloat16)
    return out.reshape(blocks, experts, BLOCK, width).transpose(1, 0, 2, 3).reshape(
        experts, tokens, width
    )


def local(out_grad, gate_prob, saved_hidden, slot_weight, pair_slot, slot_expert):
    tokens, choose = pair_slot.shape
    width = out_grad.shape[1]
    hidden_width = saved_hidden.shape[2]
    slot_count = slot_expert.shape[0]
    ep_count = lax.axis_size("ep")
    dp_count = lax.axis_size("dp")
    half = hidden_width // dp_count
    capacity = max(2, 5 * tokens * choose // (4 * slot_count))
    dp_index = lax.axis_index("dp")

    everyone = lax.all_gather(out_grad, AXES, axis=0, tiled=True)

    slots = jnp.arange(slot_count, dtype=jnp.int32)
    named = pair_slot[:, :, None] == slots[None, None, :]
    dense_gate = jnp.sum(jnp.where(named, gate_prob[:, :, None], 0.0), axis=1).T
    gates = lax.all_to_all(dense_gate, AXES, split_axis=0, concat_axis=0, tiled=True)

    expert_of_pair = jnp.sum(jnp.where(named, slot_expert[None, None, :], 0), axis=2)
    sums = combined(gate_prob, expert_of_pair, saved_hidden, ep_count)
    sums = (
        sums.reshape(ep_count, tokens, dp_count, half)
        .transpose(0, 2, 1, 3)
        .reshape(slot_count, tokens, half)
    )
    sums = lax.all_to_all(sums, AXES, split_axis=0, concat_axis=0, tiled=True)

    used = gates > 0
    before = (
        jnp.arange(tokens)[:, None] < jnp.arange(tokens)[None, :]
    ).astype(jnp.bfloat16)
    place = lax.dot_general(
        used.astype(jnp.bfloat16), before, (((1,), (0,)), ((), ())),
        preferred_element_type=jnp.float32,
    ).astype(jnp.int32)
    place = jnp.where(used, place, -1)
    select = place[:, None, :] == jnp.arange(capacity, dtype=jnp.int32)[None, :, None]
    rows = lax.dot_general(
        select.astype(jnp.bfloat16),
        everyone.reshape(slot_count, tokens, width),
        (((2,), (1,)), ((0,), (0,))),
        preferred_element_type=jnp.float32,
    )
    row_gate = jnp.sum(jnp.where(select, gates[:, None, :], 0.0), axis=2)
    pair_grad = (rows * row_gate[:, :, None]).astype(jnp.bfloat16)
    input_grads = lax.dot_general(
        pair_grad.reshape(slot_count * capacity, width),
        slot_weight[0],
        (((1,), (1,)), ((), ())),
        preferred_element_type=jnp.float32,
    ).astype(jnp.bfloat16)
    returned = lax.all_to_all(
        input_grads.reshape(slot_count, capacity, hidden_width),
        AXES, split_axis=0, concat_axis=0, tiled=True,
    )

    grad_half = lax.dot_general(
        sums.reshape(slot_count * tokens, half),
        everyone,
        (((0,), (0,)), ((), ())),
        preferred_element_type=jnp.float32,
    ).astype(jnp.bfloat16)
    rounded = lax.all_gather(grad_half, "dp", axis=0, tiled=True)
    left = (
        lax.dot_general(
            grad_half, rounded, (((1,), (1,)), ((), ())), preferred_element_type=jnp.float32
        )
        / width
    )
    width_rows = width // dp_count
    right_cols = lax.dynamic_slice_in_dim(rounded, dp_index * width_rows, width_rows, 1)
    right = (
        lax.dot_general(
            right_cols, rounded, (((0,), (0,)), ((), ())), preferred_element_type=jnp.float32
        )
        / hidden_width
    )

    served = jnp.any(named, axis=1).astype(jnp.bfloat16)
    earlier = lax.dot_general(
        before, served, (((0,), (0,)), ((), ())), preferred_element_type=jnp.float32
    ).astype(jnp.int32)
    position = jnp.sum(
        jnp.where(named, (earlier + slots * capacity)[:, None, :], 0), axis=2
    ).reshape(tokens * choose)
    pick = (
        position[:, None] == jnp.arange(slot_count * capacity, dtype=jnp.int32)[None, :]
    ).astype(jnp.bfloat16)
    hidden_grad = lax.dot_general(
        pick,
        returned.reshape(slot_count * capacity, hidden_width),
        (((1,), (0,)), ((), ())),
        preferred_element_type=jnp.float32,
    ).astype(jnp.bfloat16).reshape(tokens, choose, hidden_width)
    return (hidden_grad, left.astype(jnp.bfloat16)[None], right.astype(jnp.bfloat16)[None])


def exchange_kernel(
    ep_count, dp_count, capacity,
    grad_hbm, hidden_hbm, weight_hbm, gate_out, gate_pairs, host_pairs,
    ret_hbm, left_hbm, right_hbm,
    shards, weight, hidden, gate_in, place, sum_out, sum_in, sum_t, rows, ret_out,
    full, cols_t, left, right,
    local_sem, out_sem, o_send, o_recv, g_send, g_recv, c_send, c_recv, r_send, r_recv, x_send, x_recv,
):
    e = lax.axis_index("ep")
    c = lax.axis_index("dp")
    z, x = e // 2, e % 2
    lines = ep_count // 2
    count = ep_count * dp_count
    me = e * dp_count + c
    tokens, width = shards.shape[1:]
    hidden_width = weight.shape[0]
    half = hidden_width // dp_count

    def at(device):
        return {"ep": device // dp_count, "dp": device % dp_count}

    def index(line, column, core):
        return (line * 2 + column) * dp_count + core

    def remote(src, dst, send, recv, device):
        return pltpu.make_async_remote_copy(
            src_ref=src, dst_ref=dst, send_sem=send, recv_sem=recv,
            device_id=at(device), device_id_type=pl.DeviceIdType.MESH,
        )

    def each_peer(body):
        def step(d, carry):
            body(lax.rem(me + d, count))
            return carry
        lax.fori_loop(1, count, step, 0)

    def each_across(body):
        def step(d, carry):
            body((1 - me // (count // 2)) * (count // 2) + lax.rem(me + d, count // 2))
            return carry
        lax.fori_loop(0, count // 2, step, 0)

    def each_near(body):
        def step(d, carry):
            body(me // (count // 2) * (count // 2) + lax.rem(me + d, count // 2))
            return carry
        lax.fori_loop(1, count // 2, step, 0)

    loads = [
        pltpu.make_async_copy(grad_hbm, shards.at[me], local_sem.at[0]),
        pltpu.make_async_copy(hidden_hbm, hidden, local_sem.at[1]),
        pltpu.make_async_copy(weight_hbm, weight, local_sem.at[2]),
    ]
    for load in loads:
        load.start()

    barrier = pltpu.get_barrier_semaphore()
    each_peer(lambda peer: pl.semaphore_signal(
        barrier, inc=1, device_id=at(peer), device_id_type=pl.DeviceIdType.MESH))
    pl.semaphore_wait(barrier, count - 1)

    def gate_copy(peer):
        return remote(gate_out.at[peer], gate_in.at[me], g_send.at[peer], g_recv.at[me], peer)

    def sum_copy(peer):
        return remote(sum_out.at[peer], sum_in.at[me], c_send.at[peer], c_recv.at[me], peer)

    def ret_copy(peer):
        return remote(ret_out.at[peer], ret_hbm.at[me], r_send.at[peer], r_recv.at[me], peer)

    piece = tokens // CHUNKS

    def shard_copy(route, shard, chunk, device):
        held = shards.at[shard, pl.ds(chunk * piece, piece)]
        return remote(
            held, held, o_send.at[route, chunk, shard], o_recv.at[chunk, shard], device)

    def wait_shard(shard, chunk):
        shard_copy(0, shard, chunk, (me + 1) % count).wait_recv()

    def relay(line, chunk, action):
        shard = index(line, x, c)

        @pl.when((line <= z) & (z + 1 < lines))
        def _():
            action(shard_copy(0, shard, chunk, index(z + 1, x, c)))

        @pl.when((line >= z) & (z >= 1))
        def _():
            action(shard_copy(1, shard, chunk, index(z - 1, x, c)))

        action(shard_copy(2, shard, chunk, index(z, 1 - x, c)))
        action(shard_copy(3, shard, chunk, index(z, x, 1 - c)))

    def cross(line, chunk, action):
        action(shard_copy(3, index(line, 1 - x, c), chunk, index(z, x, 1 - c)))

    start = lambda copy: copy.start()
    each_peer(lambda peer: gate_copy(peer).start())
    loads[0].wait()
    for chunk in range(CHUNKS):
        relay(z, chunk, start)
    gate_in[me] = gate_out[me]

    loads[1].wait()
    block = gate_pairs.shape[2]
    per = tokens // gate_pairs.shape[0]
    choose = block // per
    line_of = lax.broadcasted_iota(jnp.int32, (ep_count * per, block), 0)
    lane_of = lax.broadcasted_iota(jnp.int32, (ep_count * per, block), 1)
    own = (lane_of // choose) == (line_of % per)

    def sum_block(b, carry):
        keep = own & (host_pairs[b] == line_of // per)
        exact = jnp.where(keep, gate_pairs[b], 0.0)
        high = exact.astype(jnp.bfloat16)
        low = (exact - high.astype(jnp.float32)).astype(jnp.bfloat16)
        values = hidden[pl.ds(pl.multiple_of(b * block, block), block), :]
        out = jnp.dot(high, values, preferred_element_type=jnp.float32)
        out = (out + jnp.dot(low, values, preferred_element_type=jnp.float32)).astype(jnp.bfloat16)
        for host in range(ep_count):
            for core in range(dp_count):
                sum_out[host * dp_count + core, pl.ds(pl.multiple_of(b * per, per), per), :] = out[
                    host * per:(host + 1) * per, core * half:(core + 1) * half]
        return carry

    lax.fori_loop(0, gate_pairs.shape[0], sum_block, 0)
    own_sum = pltpu.make_async_copy(sum_out.at[me], sum_in.at[me], local_sem.at[1])
    own_sum.start()

    each_peer(lambda peer: gate_copy(peer).wait_send())
    each_peer(lambda peer: remote(
        gate_out.at[peer], gate_in.at[peer], g_send.at[peer], g_recv.at[peer], peer).wait_recv())
    gates = gate_in[:, 0, :]
    used = gates > 0
    before = (
        lax.broadcasted_iota(jnp.int32, (tokens, tokens), 0)
        < lax.broadcasted_iota(jnp.int32, (tokens, tokens), 1)
    ).astype(jnp.float32).astype(jnp.bfloat16)
    earlier = jnp.dot(
        used.astype(jnp.float32).astype(jnp.bfloat16), before, preferred_element_type=jnp.float32)
    place[:, 0, :] = jnp.where(used, earlier, -1.0)
    loads[2].wait()

    rank = lax.broadcasted_iota(jnp.int32, (capacity, tokens), 0).astype(jnp.float32)
    tile = 256

    def serve(line):
        first = index(line, 0, 0)
        number = 2 * dp_count

        def gather(i, carry):
            shard = first + i
            select = place[shard] == rank
            picked = jnp.dot(
                jnp.where(select, 1.0, 0.0).astype(jnp.bfloat16), shards[shard],
                preferred_element_type=jnp.float32)
            gate = jnp.sum(jnp.where(select, gate_in[shard], 0.0), axis=1, keepdims=True)
            rows[i] = (picked * gate).astype(jnp.bfloat16)
            return carry

        lax.fori_loop(0, number, gather, 0)

        def product(n, carry):
            lanes = pl.ds(pl.multiple_of(n * tile, tile), tile)
            out = lax.dot_general(
                rows[...].reshape(number * capacity, width), weight[lanes, :],
                (((1,), (1,)), ((), ())), preferred_element_type=jnp.float32)
            ret_out[pl.ds(first, number), :, lanes] = out.astype(jnp.bfloat16).reshape(
                number, capacity, tile)
            return carry

        lax.fori_loop(0, hidden_width // tile, product, 0)

        def send(i, carry):
            shard = first + i

            @pl.when(shard != me)
            def _():
                ret_copy(shard).start()

            @pl.when(shard == me)
            def _():
                pltpu.make_async_copy(ret_out.at[me], ret_hbm.at[me], local_sem.at[0]).start()

            return carry

        lax.fori_loop(0, number, send, 0)

    def inside(line, chunk, body):
        @pl.when((line >= 0) & (line < lines))
        def _():
            body(line, chunk)

    def take_line(line, chunk):
        wait_shard(index(line, x, c), chunk)
        relay(line, chunk, start)

    def take_cross(line, chunk):
        wait_shard(index(line, 1 - x, c), chunk)
        cross(line, chunk, start)

    side = 1 - 2 * (z // 2)
    second = z + side
    fourth = 3 * (1 - z // 2)
    order = [z, second, 6 - z - second - fourth, fourth]
    def both(line_below, line_above, chunk, body):
        inside(line_below, chunk, body)
        inside(line_above, chunk, body)

    for event, level in PLAN:
        if event == "across":
            each_across(lambda peer: sum_copy(peer).start())
        elif event == "near":
            each_near(lambda peer: sum_copy(peer).start())
        elif event == "serve":
            line = order[level]
            for chunk in range(CHUNKS):
                wait_shard(index(line, 0, 1 - c), chunk)
                wait_shard(index(line, 1, 1 - c), chunk)
            serve(line)
        else:
            for chunk in range(CHUNKS):
                if "line" in event:
                    both(z - level, z + level, chunk, take_line)
                if "cross" in event:
                    if level == 1:
                        take_cross(z, chunk)
                    else:
                        both(z - level + 1, z + level - 1, chunk, take_cross)

    own_sum.wait()
    each_peer(lambda peer: remote(
        sum_out.at[peer], sum_in.at[peer], c_send.at[peer], c_recv.at[peer], peer).wait_recv())

    def turn(j, carry):
        sum_t[:, pl.ds(pl.multiple_of(j * tokens, tokens), tokens)] = sum_in[j].T
        return carry

    lax.fori_loop(0, count, turn, 0)
    mine = pl.ds(pl.multiple_of(c * half, half), half)

    def grad_tile(n, carry):
        lanes = pl.ds(pl.multiple_of(n * tile, tile), tile)
        full[mine, lanes] = jnp.dot(
            sum_t[...], shards[:, :, lanes].reshape(count * tokens, tile),
            preferred_element_type=jnp.float32).astype(jnp.bfloat16)
        return carry

    lax.fori_loop(0, width // tile, grad_tile, 0)
    swap = remote(full.at[mine], full.at[mine], x_send, x_recv, index(z, x, 1 - c))
    swap.start()
    swap.wait()

    part = width // dp_count
    cols_t[...] = full[:, pl.ds(pl.multiple_of(c * part, part), part)].T
    left[...] = (
        lax.dot_general(
            full[mine, :], full[...], (((1,), (1,)), ((), ())), preferred_element_type=jnp.float32)
        / width
    ).astype(jnp.bfloat16)
    left_copy = pltpu.make_async_copy(left, left_hbm, out_sem.at[0])
    left_copy.start()

    def right_tile(n, carry):
        lanes = pl.ds(pl.multiple_of(n * tile, tile), tile)
        right[:, lanes] = (
            jnp.dot(cols_t[...], full[:, lanes], preferred_element_type=jnp.float32) / hidden_width
        ).astype(jnp.bfloat16)
        return carry

    lax.fori_loop(0, width // tile, right_tile, 0)
    right_copy = pltpu.make_async_copy(right, right_hbm, out_sem.at[1])
    right_copy.start()

    each_peer(lambda peer: remote(
        ret_out.at[peer], ret_hbm.at[peer], r_send.at[peer], r_recv.at[peer], peer).wait_recv())
    pltpu.make_async_copy(ret_out.at[me], ret_hbm.at[me], local_sem.at[0]).wait()
    each_peer(lambda peer: sum_copy(peer).wait_send())
    each_peer(lambda peer: ret_copy(peer).wait_send())
    wait_send = lambda copy: copy.wait_send()
    for chunk in range(CHUNKS):
        for line in range(lines):
            relay(line, chunk, wait_send)
            cross(line, chunk, wait_send)
    left_copy.wait()
    right_copy.wait()


def exchange(out_grad, saved_hidden, weight, dense_gate, gate_pairs, host_pairs, ep_count, dp_count, capacity):
    tokens, width = out_grad.shape
    pairs, hidden_width = saved_hidden.shape
    count = ep_count * dp_count
    half, part = hidden_width // dp_count, width // dp_count
    bf16, f32 = jnp.bfloat16, jnp.float32
    dma = pltpu.SemaphoreType.DMA
    anywhere = pl.BlockSpec(memory_space=pl.ANY)
    vmem = pl.BlockSpec(memory_space=pltpu.VMEM)
    return pl.pallas_call(
        functools.partial(exchange_kernel, ep_count, dp_count, capacity),
        out_shape=(
            jax.ShapeDtypeStruct((count, capacity, hidden_width), bf16),
            jax.ShapeDtypeStruct((half, hidden_width), bf16),
            jax.ShapeDtypeStruct((part, width), bf16),
        ),
        in_specs=[anywhere] * 3 + [vmem] * 3,
        out_specs=(anywhere,) * 3,
        scratch_shapes=[
            pltpu.VMEM((count, tokens, width), bf16),
            pltpu.VMEM((hidden_width, width), bf16),
            pltpu.VMEM((pairs, hidden_width), bf16),
            pltpu.VMEM((count, 1, tokens), f32),
            pltpu.VMEM((count, 1, tokens), f32),
            pltpu.VMEM((count, tokens, half), bf16),
            pltpu.VMEM((count, tokens, half), bf16),
            pltpu.VMEM((half, count * tokens), bf16),
            pltpu.VMEM((2 * dp_count, capacity, width), bf16),
            pltpu.VMEM((count, capacity, hidden_width), bf16),
            pltpu.VMEM((hidden_width, width), bf16),
            pltpu.VMEM((part, hidden_width), bf16),
            pltpu.VMEM((half, hidden_width), bf16),
            pltpu.VMEM((part, width), bf16),
            dma((3,)), dma((2,)), dma((4, CHUNKS, count)), dma((CHUNKS, count)), dma((count,)), dma((count,)),
            dma((count,)), dma((count,)), dma((count,)), dma((count,)), dma, dma,
        ],
        compiler_params=pltpu.CompilerParams(
            collective_id=0, has_side_effects=True, vmem_limit_bytes=56 << 20),
        cost_estimate=pl.CostEstimate(
            flops=16_000_000_000, bytes_accessed=20_000_000, transcendentals=0),
    )(out_grad, saved_hidden, weight, dense_gate, gate_pairs, host_pairs)


def restore(returned, named, before, capacity):
    tokens, choose, slot_count = named.shape
    hidden_width = returned.shape[2]
    slots = jnp.arange(slot_count, dtype=jnp.int32)
    served = jnp.any(named, axis=1).astype(jnp.bfloat16)
    earlier = lax.dot_general(
        before, served, (((0,), (0,)), ((), ())), preferred_element_type=jnp.float32
    ).astype(jnp.int32)
    position = jnp.sum(
        jnp.where(named, (earlier + slots * capacity)[:, None, :], 0), axis=2
    ).reshape(tokens * choose)
    pick = (
        position[:, None] == jnp.arange(slot_count * capacity, dtype=jnp.int32)[None, :]
    ).astype(jnp.bfloat16)
    return lax.dot_general(
        pick,
        returned.reshape(slot_count * capacity, hidden_width),
        (((1,), (0,)), ((), ())),
        preferred_element_type=jnp.float32,
    ).astype(jnp.bfloat16).reshape(tokens, choose, hidden_width)


def fused(out_grad, gate_prob, saved_hidden, slot_weight, pair_slot, slot_expert):
    tokens, choose = pair_slot.shape
    slot_count = slot_expert.shape[0]
    ep_count = lax.axis_size("ep")
    dp_count = lax.axis_size("dp")
    capacity = max(2, 5 * tokens * choose // (4 * slot_count))
    slots = jnp.arange(slot_count, dtype=jnp.int32)
    named = pair_slot[:, :, None] == slots[None, None, :]
    dense_gate = jnp.sum(jnp.where(named, gate_prob[:, :, None], 0.0), axis=1).T
    expert_of_pair = jnp.sum(jnp.where(named, slot_expert[None, None, :], 0), axis=2)
    blocks = tokens // BLOCK
    returned, left, right = exchange(
        out_grad,
        saved_hidden.reshape(tokens * choose, saved_hidden.shape[2]),
        slot_weight[0],
        dense_gate[:, None, :],
        gate_prob.reshape(blocks, 1, BLOCK * choose),
        expert_of_pair.reshape(blocks, 1, BLOCK * choose),
        ep_count, dp_count, capacity,
    )
    before = (
        jnp.arange(tokens)[:, None] < jnp.arange(tokens)[None, :]
    ).astype(jnp.bfloat16)
    return restore(returned, named, before, capacity), left[None], right[None]


def solution(mesh):
    fits = mesh.shape["ep"] == 8 and mesh.shape["dp"] == 2
    return jax.shard_map(
        fused if fits else local,
        mesh=mesh,
        in_specs=(
            P(("groups", "ep", "dp"), None),
            P(("groups", "ep", "dp"), None),
            P(("groups", "ep", "dp"), None, None),
            P(("ep", "dp"), None, None),
            P(("groups", "ep", "dp"), None),
            P("groups"),
        ),
        out_specs=(
            P(("groups", "ep", "dp"), None, None),
            P(("groups", "ep"), "dp", None),
            P(("groups", "ep"), "dp", None),
        ),
        check_vma=False,
    )
```
